32 devices in a mesh: blk: 8 (over z, core), group: 4 (over y, x).
Axes of the slice: x: 2, y: 2, z: 4, core: 2. Of those that a mesh axis runs over, the one named last changes fastest.
Arguments:
- img_feat: bfloat16 [4096, 3072], P(('blk', 'group')), may hold values from -0.375 to 0.375
- head_weight: bfloat16 [3072, 512], replicated, may hold values from -1 to 3
- text_emb: bfloat16 [4096, 512], P(('blk', 'group')), may hold values from -0.375 to 0.375
- natural_exponent_factor: float32 [1], replicated, may hold values from 1.6 to 2
- bias: float32 [1], replicated, may hold values from -3.5 to -2.5
Outputs:
- d_feat: float32 [4096, 3072], P(('blk', 'group'))
- d_text: float32 [4096, 512], P(('blk', 'group'))
The draws below stay inside these ranges and needn't reach their ends.
All inputs are finite; a program needn't handle non-finite values.
Results may differ from the reference program's by a relative error of at most 0.005.
Values may be sent and summed in bfloat16 or wider, within the bound.
No kernel may reach another device: no remote copies, remote signals or barrier semaphores. Data moves between devices by JAX's collectives and lax.ppermute only.
A program may use at most 64 MiB of HBM per device.

```python
import math
import jax
import jax.numpy as jnp
from jax import lax

EMB = 512
IMG_WIDTH = 3072
ROWS_DEV = 128
STEPS = 2
BATCH = 4096
N_BLK = 8
N_GROUP = 4


def shared_rows(key):
    base = jax.random.fold_in(key, 7101)
    centres = jax.random.normal(jax.random.fold_in(base, 1), (64, EMB), jnp.float32)
    first_ids = jax.random.randint(jax.random.fold_in(base, 2), (BATCH,), 0, 64)
    second_ids = jax.random.randint(jax.random.fold_in(base, 3), (BATCH,), 0, 64)
    first_coef = jax.random.normal(jax.random.fold_in(base, 4), (BATCH, 1), jnp.float32)
    second_coef = jax.random.normal(jax.random.fold_in(base, 5), (BATCH, 1), jnp.float32)
    own_part = jax.random.normal(jax.random.fold_in(base, 6), (BATCH, EMB), jnp.float32)
    mixed = first_coef * jnp.take(centres, first_ids, axis=0) + second_coef * jnp.take(centres, second_ids, axis=0)
    return 0.5477 * mixed + 0.6325 * own_part


def noise_and_scales(key, rows, columns):
    noise = jnp.clip(jax.random.normal(jax.random.fold_in(key, 1), (rows, columns), jnp.float32), -6.0, 6.0)
    scales = jnp.ones((rows, 1), jnp.float32)
    return (noise, scales)


def draw_img_feat(key, part):
    latent = shared_rows(key)
    noise, scales = noise_and_scales(jax.random.fold_in(key, 7202), BATCH, IMG_WIDTH)
    leading = latent + 0.5 * noise[:, :EMB]
    values = jnp.concatenate([leading, noise[:, EMB:]], axis=1)
    return jnp.clip(0.03125 * scales * values, -0.375, 0.375).astype(jnp.bfloat16)


def draw_text_emb(key, part):
    latent = shared_rows(key)
    noise, scales = noise_and_scales(jax.random.fold_in(key, 7303), BATCH, EMB)
    values = latent + 1.2 * noise
    return jnp.clip(0.03125 * scales * values, -0.375, 0.375).astype(jnp.bfloat16)


def draw_head_weight(key, part):
    base = jax.random.fold_in(key, 7404)
    noise = jnp.clip(jax.random.normal(base, (IMG_WIDTH, EMB), jnp.float32), -4.0, 4.0)
    row_index = jax.lax.broadcasted_iota(jnp.int32, (IMG_WIDTH, EMB), 0)
    col_index = jax.lax.broadcasted_iota(jnp.int32, (IMG_WIDTH, EMB), 1)
    leading = jnp.where(row_index == col_index, 2.0, 0.0).astype(jnp.float32)
    values = leading + noise / math.sqrt(IMG_WIDTH)
    return jnp.clip(values, -1.0, 3.0).astype(jnp.bfloat16)


def setup_inputs(seed: int = 0) -> dict:
    keys = jax.random.split(jax.random.key(seed), 6)
    img_feat = draw_img_feat(jax.random.fold_in(keys[5], 71), 0)
    head_weight = draw_head_weight(jax.random.fold_in(keys[5], 71), 0)
    text_emb = draw_text_emb(jax.random.fold_in(keys[5], 71), 0)
    natural_exponent_factor = jnp.clip(jax.random.uniform(keys[3], (1,), jnp.float32, 1.6, 2.0), 1.6, 2.0)
    bias = jnp.clip(jax.random.uniform(keys[4], (1,), jnp.float32, -3.5, -2.5), -3.5, -2.5)
    return {"img_feat": img_feat, "head_weight": head_weight, "text_emb": text_emb, "natural_exponent_factor": natural_exponent_factor, "bias": bias}


EPS = 1e-06

def to_unit(values):
    inverse = lax.rsqrt(lax.optimization_barrier(jnp.sum(values * values, axis=-1, keepdims=True)) + EPS)
    return (values * inverse, inverse)

def unit_back(grad_in, unit_rows, inverse):
    return (grad_in - unit_rows * lax.optimization_barrier(jnp.sum(unit_rows * grad_in, axis=-1, keepdims=True))) * inverse

def reference(img_feat, head_weight, text_emb, natural_exponent_factor, bias):
    similarity_multiplier = jnp.exp(natural_exponent_factor[0])
    partner_offset = bias[0]
    projected = jnp.dot(img_feat, head_weight, preferred_element_type=jnp.float32)
    img_unit, img_inv = to_unit(projected)
    txt_unit, txt_inv = to_unit(text_emb.astype(jnp.float32))
    panel_rows = ROWS_DEV * N_GROUP
    img_blocks = img_unit.astype(jnp.bfloat16).reshape(N_BLK, panel_rows, EMB).astype(jnp.float32)
    txt_blocks = txt_unit.astype(jnp.bfloat16).reshape(N_BLK, panel_rows, EMB).astype(jnp.float32)
    row_ids = lax.broadcasted_iota(jnp.int32, (panel_rows, panel_rows), 0)
    col_ids = lax.broadcasted_iota(jnp.int32, (panel_rows, panel_rows), 1)
    diagonal_mask = jnp.where(row_ids == col_ids, 1.0, 0.0).astype(jnp.float32)
    grad_img = jnp.zeros((N_BLK, panel_rows, EMB), jnp.float32)
    grad_txt = jnp.zeros((N_BLK, panel_rows, EMB), jnp.float32)
    for loop_step in range(STEPS):
        rolled = jnp.roll(txt_blocks, loop_step, axis=0)
        positive = diagonal_mask if loop_step == 0 else jnp.zeros_like(diagonal_mask)

        def block_terms(pair):
            picture_solo_vector, caption_solo_vector = pair
            matched_similarity_matrix = similarity_multiplier * jnp.dot(picture_solo_vector, caption_solo_vector.T, precision=lax.Precision.HIGHEST) + partner_offset
            weights_low = (jax.nn.sigmoid(matched_similarity_matrix) - positive).astype(jnp.bfloat16)
            weights_low = lax.optimization_barrier(weights_low)
            factor_matrix_expanded = weights_low.astype(jnp.float32)
            picture_addend = similarity_multiplier * jnp.dot(factor_matrix_expanded, caption_solo_vector, precision=lax.Precision.HIGHEST)
            caption_addend = similarity_multiplier * jnp.dot(factor_matrix_expanded.T, picture_solo_vector, precision=lax.Precision.HIGHEST)
            return (picture_addend, caption_addend)
        img_terms, txt_terms = lax.map(block_terms, (img_blocks, rolled))
        grad_img = grad_img + img_terms
        grad_txt = grad_txt + jnp.roll(txt_terms, -loop_step, axis=0)
    grad_img = grad_img.reshape(N_BLK * panel_rows, EMB)
    grad_txt = grad_txt.reshape(N_BLK * panel_rows, EMB)
    img_back = unit_back(grad_img, img_unit, img_inv).astype(jnp.bfloat16)
    d_feat = lax.dot_general(img_back, head_weight, (((1,), (1,)), ((), ())), preferred_element_type=jnp.float32)
    d_text = unit_back(grad_txt, txt_unit, txt_inv)
    return (d_feat, d_text)
```

```python
import functools

import jax
import jax.numpy as jnp
from jax import lax
from jax.experimental import pallas as pl
from jax.experimental.pallas import tpu as pltpu
from jax.sharding import PartitionSpec as P

EPS = 1e-06
F32 = jnp.float32
BF16 = jnp.bfloat16
CONTRACT_LAST = (((1,), (1,)), ((), ()))
VMEM = pl.BlockSpec(memory_space=pltpu.VMEM)
SMEM = pl.BlockSpec(memory_space=pltpu.SMEM)


def to_unit(values):
    inverse = lax.rsqrt(jnp.sum(values * values, axis=-1, keepdims=True) + EPS)
    return values * inverse, inverse


def unit_back(grad_in, unit_rows, inverse):
    return (grad_in - unit_rows * jnp.sum(unit_rows * grad_in, axis=-1, keepdims=True)) * inverse


def project_kernel(img_ref, head_ref, unit_ref, inv_ref, low_ref):
    projected = jnp.dot(img_ref[...], head_ref[...], preferred_element_type=F32)
    unit, inverse = to_unit(projected)
    unit_ref[...] = unit
    inv_ref[...] = inverse
    low_ref[...] = unit.astype(BF16)


def meet(scale, bias, left, right, rows):
    z = scale * lax.dot_general(left, right, CONTRACT_LAST, preferred_element_type=F32) + bias
    row_ids = lax.broadcasted_iota(jnp.int32, z.shape, 0)
    col_ids = lax.broadcasted_iota(jnp.int32, z.shape, 1)
    positive = jnp.where((row_ids == col_ids) & (row_ids < rows), 1.0, 0.0)
    weight = (1.0 / (1.0 + jnp.exp(-z)) - positive).astype(BF16)
    return scale * jnp.dot(weight, right, preferred_element_type=F32)


def image_kernel(factor_ref, bias_ref, own_ref, visit_ref, *refs):
    text_refs, (grad_ref, back_ref) = refs[:-2], refs[-2:]
    rows = own_ref.shape[0]
    texts = jnp.concatenate([to_unit(ref[...].astype(F32))[0].astype(BF16) for ref in text_refs], axis=0)
    left = jnp.concatenate([own_ref[...], visit_ref[...]], axis=0)
    scale = jnp.exp(jnp.full((1, 1), factor_ref[0], F32))
    grad = meet(scale, bias_ref[0], left, texts, rows)
    grad_ref[...] = grad[:rows]
    back_ref[...] = grad[rows:].astype(BF16)


def text_kernel(factor_ref, bias_ref, own_ref, visit_ref, *refs):
    image_refs, (grad_ref, back_ref) = refs[:-2], refs[-2:]
    rows = own_ref.shape[0]
    images = jnp.concatenate([ref[...] for ref in image_refs], axis=0)
    left = jnp.concatenate(
        [to_unit(ref[...].astype(F32))[0].astype(BF16) for ref in (own_ref, visit_ref)], axis=0
    )
    scale = jnp.exp(jnp.full((1, 1), factor_ref[0], F32))
    grad = meet(scale, bias_ref[0], left, images, rows)
    grad_ref[...] = grad[:rows]
    back_ref[...] = grad[rows:].astype(BF16)


def feat_kernel(grad_ref, back_ref, unit_ref, inv_ref, head_ref, out_ref, low_ref):
    @pl.when(pl.program_id(0) == 0)
    def _():
        grad = grad_ref[...] + back_ref[...].astype(F32)
        low_ref[...] = unit_back(grad, unit_ref[...], inv_ref[...]).astype(BF16)

    out_ref[...] = lax.dot_general(low_ref[...], head_ref[...], CONTRACT_LAST, preferred_element_type=F32)


def text_out_kernel(grad_ref, back_ref, text_ref, out_ref):
    unit, inverse = to_unit(text_ref[...].astype(F32))
    out_ref[...] = unit_back(grad_ref[...] + back_ref[...].astype(F32), unit, inverse)


def body(img_feat, head_weight, text_emb, natural_exponent_factor, bias):
    rows, width = img_feat.shape
    emb = text_emb.shape[1]
    n_blk, n_group = lax.axis_size("blk"), lax.axis_size("group")
    shape = jax.ShapeDtypeStruct
    sub = functools.partial(pl.pallas_call)

    def to_peer(piece, k):
        if n_group & (n_group - 1) == 0:
            route = [(i, i ^ k) for i in range(n_group)]
        else:
            route = [(i, (i + k) % n_group) for i in range(n_group)]
        return lax.ppermute(piece, "group", route)

    def to_block(piece, distance):
        return lax.ppermute(piece, "blk", [(i, (i + distance) % n_blk) for i in range(n_blk)])

    texts = [text_emb] + [to_peer(text_emb, k) for k in range(1, n_group)]
    text_visit = to_block(text_emb, 1)

    img_unit, img_inv, img_low = sub(
        project_kernel,
        out_shape=(shape((rows, emb), F32), shape((rows, 1), F32), shape((rows, emb), BF16)),
        in_specs=[VMEM] * 2,
        out_specs=(VMEM,) * 3,
    )(img_feat, head_weight)

    img_visit = to_block(img_low, -1)
    images = [img_low] + [to_peer(img_low, k) for k in range(1, n_group)]

    pair = (shape((rows, emb), F32), shape((rows, emb), BF16))
    grad_img, img_return = sub(
        image_kernel,
        out_shape=pair,
        in_specs=[SMEM] * 2 + [VMEM] * (2 + n_group),
        out_specs=(VMEM,) * 2,
    )(natural_exponent_factor, bias, img_low, img_visit, *texts)
    img_back = to_block(img_return, 1)

    grad_txt, txt_return = sub(
        text_kernel,
        out_shape=pair,
        in_specs=[SMEM] * 2 + [VMEM] * (2 + n_group),
        out_specs=(VMEM,) * 2,
    )(natural_exponent_factor, bias, text_emb, text_visit, *images)
    txt_back = to_block(txt_return, -1)

    tile = 768 if width % 768 == 0 else width
    whole = lambda *dims: pl.BlockSpec(dims, lambda j: (0, 0))
    d_feat = sub(
        feat_kernel,
        grid=(width // tile,),
        out_shape=shape((rows, width), F32),
        in_specs=[
            whole(rows, emb),
            whole(rows, emb),
            whole(rows, emb),
            whole(rows, 1),
            pl.BlockSpec((tile, emb), lambda j: (j, 0)),
        ],
        out_specs=pl.BlockSpec((rows, tile), lambda j: (0, j)),
        scratch_shapes=[pltpu.VMEM((rows, emb), BF16)],
    )(grad_img, img_back, img_unit, img_inv, head_weight)

    d_text = sub(
        text_out_kernel, out_shape=shape((rows, emb), F32), in_specs=[VMEM] * 3, out_specs=VMEM
    )(grad_txt, txt_back, text_emb)
    return d_feat, d_text


def solution(mesh):
    return jax.shard_map(
        body,
        mesh=mesh,
        in_specs=(P(("blk", "group"), None), P(), P(("blk", "group"), None), P(), P()),
        out_specs=(P(("blk", "group"), None), P(("blk", "group"), None)),
        check_vma=False,
    )
```

```python
import functools

import jax
import jax.numpy as jnp
from jax import lax
from jax.experimental import pallas as pl
from jax.experimental.pallas import tpu as pltpu
from jax.sharding import PartitionSpec as P

EPS = 1e-06
F32 = jnp.float32
BF16 = jnp.bfloat16
CONTRACT_LAST = (((1,), (1,)), ((), ()))
VMEM = pl.BlockSpec(memory_space=pltpu.VMEM)
SMEM = pl.BlockSpec(memory_space=pltpu.SMEM)


def to_unit(values):
    inverse = lax.rsqrt(jnp.sum(values * values, axis=-1, keepdims=True) + EPS)
    return values * inverse, inverse


def unit_back(grad_in, unit_rows, inverse):
    return (grad_in - unit_rows * jnp.sum(unit_rows * grad_in, axis=-1, keepdims=True)) * inverse


def project_kernel(img_ref, head_ref, unit_ref, inv_ref, low_ref):
    projected = jnp.dot(img_ref[...], head_ref[...], preferred_element_type=F32)
    unit, inverse = to_unit(projected)
    unit_ref[...] = unit
    inv_ref[...] = inverse
    low_ref[...] = unit.astype(BF16)


def meet(scale, bias, left, right, rows):
    z = scale * lax.dot_general(left, right, CONTRACT_LAST, preferred_element_type=F32) + bias
    row_ids = lax.broadcasted_iota(jnp.int32, z.shape, 0)
    col_ids = lax.broadcasted_iota(jnp.int32, z.shape, 1)
    positive = jnp.where((row_ids == col_ids) & (row_ids < rows), 1.0, 0.0)
    weight = (1.0 / (1.0 + jnp.exp(-z)) - positive).astype(BF16)
    return scale * jnp.dot(weight, right, preferred_element_type=F32)


def image_kernel(factor_ref, bias_ref, own_ref, visit_ref, *refs):
    text_refs, (grad_ref, back_ref) = refs[:-2], refs[-2:]
    rows = own_ref.shape[0]
    texts = jnp.concatenate([to_unit(ref[...].astype(F32))[0].astype(BF16) for ref in text_refs], axis=0)
    left = jnp.concatenate([own_ref[...], visit_ref[...]], axis=0)
    scale = jnp.exp(jnp.full((1, 1), factor_ref[0], F32))
    grad = meet(scale, bias_ref[0], left, texts, rows)
    grad_ref[...] = grad[:rows]
    back_ref[...] = grad[rows:].astype(BF16)


def text_kernel(factor_ref, bias_ref, own_ref, visit_ref, *refs):
    image_refs, (grad_ref, back_ref) = refs[:-2], refs[-2:]
    rows = own_ref.shape[0]
    images = jnp.concatenate([ref[...] for ref in image_refs], axis=0)
    left = jnp.concatenate(
        [to_unit(ref[...].astype(F32))[0].astype(BF16) for ref in (own_ref, visit_ref)], axis=0
    )
    scale = jnp.exp(jnp.full((1, 1), factor_ref[0], F32))
    grad = meet(scale, bias_ref[0], left, images, rows)
    grad_ref[...] = grad[:rows]
    back_ref[...] = grad[rows:].astype(BF16)


def feat_kernel(grad_ref, back_ref, unit_ref, inv_ref, head_ref, out_ref, low_ref):
    @pl.when(pl.program_id(0) == 0)
    def _():
        grad = grad_ref[...] + back_ref[...].astype(F32)
        low_ref[...] = unit_back(grad, unit_ref[...], inv_ref[...]).astype(BF16)

    out_ref[...] = lax.dot_general(low_ref[...], head_ref[...], CONTRACT_LAST, preferred_element_type=F32)


def text_out_kernel(grad_ref, back_ref, text_ref, out_ref):
    unit, inverse = to_unit(text_ref[...].astype(F32))
    out_ref[...] = unit_back(grad_ref[...] + back_ref[...].astype(F32), unit, inverse)


def body(img_feat, head_weight, text_emb, natural_exponent_factor, bias):
    rows, width = img_feat.shape
    emb = text_emb.shape[1]
    n_blk, n_group = lax.axis_size("blk"), lax.axis_size("group")
    shape = jax.ShapeDtypeStruct
    sub = functools.partial(
        pl.pallas_call, compiler_params=pltpu.CompilerParams(vmem_limit_bytes=16 * 2**20)
    )

    def cost(flops, moved):
        return pl.CostEstimate(flops=flops, bytes_accessed=moved, transcendentals=0)

    def to_peer(piece, k):
        if n_group & (n_group - 1) == 0:
            route = [(i, i ^ k) for i in range(n_group)]
        else:
            route = [(i, (i + k) % n_group) for i in range(n_group)]
        return lax.ppermute(piece, "group", route)

    def to_block(piece, distance):
        return lax.ppermute(piece, "blk", [(i, (i + distance) % n_blk) for i in range(n_blk)])

    texts = [text_emb] + [to_peer(text_emb, k) for k in range(1, n_group)]
    text_visit = to_block(text_emb, 1)

    img_unit, img_inv, img_low = sub(
        project_kernel,
        cost_estimate=cost(2 * rows * width * emb, 2 * width * (rows + emb)),
        out_shape=(shape((rows, emb), F32), shape((rows, 1), F32), shape((rows, emb), BF16)),
        in_specs=[VMEM] * 2,
        out_specs=(VMEM,) * 3,
    )(img_feat, head_weight)

    img_visit = to_block(img_low, -1)
    images = [img_low] + [to_peer(img_low, k) for k in range(1, n_group)]

    pair = (shape((rows, emb), F32), shape((rows, emb), BF16))
    grad_img, img_return = sub(
        image_kernel,
        cost_estimate=cost(8 * rows * rows * n_group * emb, 4 * rows * emb * (n_group + 4)),
        out_shape=pair,
        in_specs=[SMEM] * 2 + [VMEM] * (2 + n_group),
        out_specs=(VMEM,) * 2,
    )(natural_exponent_factor, bias, img_low, img_visit, *texts)
    img_back = to_block(img_return, 1)

    grad_txt, txt_return = sub(
        text_kernel,
        cost_estimate=cost(8 * rows * rows * n_group * emb, 4 * rows * emb * (n_group + 4)),
        out_shape=pair,
        in_specs=[SMEM] * 2 + [VMEM] * (2 + n_group),
        out_specs=(VMEM,) * 2,
    )(natural_exponent_factor, bias, text_emb, text_visit, *images)
    txt_back = to_block(txt_return, -1)

    tile = 768 if width % 768 == 0 else width
    whole = lambda *dims: pl.BlockSpec(dims, lambda j: (0, 0))
    d_feat = sub(
        feat_kernel,
        cost_estimate=cost(2 * rows * width * emb, 4 * width * (rows + emb)),
        grid=(width // tile,),
        out_shape=shape((rows, width), F32),
        in_specs=[
            whole(rows, emb),
            whole(rows, emb),
            whole(rows, emb),
            whole(rows, 1),
            pl.BlockSpec((tile, emb), lambda j: (j, 0)),
        ],
        out_specs=pl.BlockSpec((rows, tile), lambda j: (0, j)),
        scratch_shapes=[pltpu.VMEM((rows, emb), BF16)],
    )(grad_img, img_back, img_unit, img_inv, head_weight)

    d_text = sub(
        text_out_kernel, out_shape=shape((rows, emb), F32), in_specs=[VMEM] * 3, out_specs=VMEM
    )(grad_txt, txt_back, text_emb)
    return d_feat, d_text


def solution(mesh):
    return jax.shard_map(
        body,
        mesh=mesh,
        in_specs=(P(("blk", "group"), None), P(), P(("blk", "group"), None), P(), P()),
        out_specs=(P(("blk", "group"), None), P(("blk", "group"), None)),
        check_vma=False,
    )
```

```python
import functools
import math

import jax
import jax.numpy as jnp
from jax import lax
from jax.experimental import pallas as pl
from jax.experimental.pallas import tpu as pltpu
from jax.sharding import PartitionSpec as P

EPS = 1e-06
F32 = jnp.float32
BF16 = jnp.bfloat16
CONTRACT_LAST = (((1,), (1,)), ((), ()))
VMEM = pl.BlockSpec(memory_space=pltpu.VMEM)
SMEM = pl.BlockSpec(memory_space=pltpu.SMEM)
ANY = pl.BlockSpec(memory_space=pl.ANY)
HBM = pl.BlockSpec(memory_space=pltpu.HBM)


def to_unit(values):
    inverse = lax.rsqrt(jnp.sum(values * values, axis=-1, keepdims=True) + EPS)
    return values * inverse, inverse


def unit_back(grad_in, unit_rows, inverse):
    return (grad_in - unit_rows * jnp.sum(unit_rows * grad_in, axis=-1, keepdims=True)) * inverse


def text_kernel(text_ref, unit_ref, inv_ref, low_ref):
    unit, inverse = to_unit(text_ref[...].astype(F32))
    unit_ref[...] = unit
    inv_ref[...] = inverse
    low_ref[...] = unit.astype(BF16)


def project_kernel(img_ref, head_ref, unit_ref, inv_ref, low_ref):
    projected = jnp.dot(img_ref[...], head_ref[...], preferred_element_type=F32)
    unit, inverse = to_unit(projected)
    unit_ref[...] = unit
    inv_ref[...] = inverse
    low_ref[...] = unit.astype(BF16)


def meet(scale, bias, left, right, rows):
    z = scale * lax.dot_general(left, right, CONTRACT_LAST, preferred_element_type=F32) + bias
    row_ids = lax.broadcasted_iota(jnp.int32, z.shape, 0)
    col_ids = lax.broadcasted_iota(jnp.int32, z.shape, 1)
    positive = jnp.where((row_ids == col_ids) & (row_ids < rows), 1.0, 0.0)
    weight = (1.0 / (1.0 + jnp.exp(-z)) - positive).astype(BF16)
    return scale * jnp.dot(weight, right, preferred_element_type=F32)


def meet_kernel(n_left, factor_ref, bias_ref, after_ref, *refs):
    left_refs, refs = refs[:n_left], refs[n_left:]
    right_refs, (grad_ref, *out_refs) = refs[:-n_left], refs[-n_left:]
    rows = grad_ref.shape[0]
    left = jnp.concatenate([ref[...] for ref in left_refs], axis=0)
    right = jnp.concatenate([ref[...] for ref in right_refs], axis=0)
    scale = jnp.exp(factor_ref[...])
    grad = meet(scale, bias_ref[...], left, right, rows)
    grad_ref[...] = grad[:rows]
    for k, ref in enumerate(out_refs, 1):
        ref[...] = grad[k * rows : (k + 1) * rows].astype(BF16)


def feat_kernel(grad_ref, unit_ref, inv_ref, head_ref, *refs):
    peer_refs, (out_ref, flag_ref, out_here, sems) = refs[:-4], refs[-4:]
    parts = sems.shape[0]
    width = head_ref.shape[0] // parts
    grad = grad_ref[...]
    for ref in peer_refs:
        grad += ref[...].astype(F32)
    low = unit_back(grad, unit_ref[...], inv_ref[...]).astype(BF16)
    copies = []
    for i in range(parts):
        span = pl.ds(i * width, width)
        out_here[:, span] = lax.dot_general(low, head_ref[span], CONTRACT_LAST, preferred_element_type=F32)
        copy = pltpu.make_async_copy(out_here.at[:, span], out_ref.at[:, span], sems.at[i])
        copy.start()
        copies.append(copy)
    for copy in copies:
        copy.wait()
    flag_ref[...] = jnp.zeros_like(flag_ref)


def text_out_kernel(after_ref, grad_ref, unit_ref, inv_ref, *refs):
    peer_refs, out_ref = refs[:-1], refs[-1]
    grad = grad_ref[...]
    for ref in peer_refs:
        grad += ref[...].astype(F32)
    out_ref[...] = unit_back(grad, unit_ref[...], inv_ref[...])


def body(img_feat, head_weight, text_emb, natural_exponent_factor, bias):
    rows, width = img_feat.shape
    emb = text_emb.shape[1]
    n_blk, n_group = lax.axis_size("blk"), lax.axis_size("group")
    n_col = next(k for k in range(math.isqrt(n_group), 0, -1) if n_group % k == 0)
    n_row = n_group // n_col
    shape = jax.ShapeDtypeStruct
    parts = 4 if width % 512 == 0 else 1

    def kernel(body, flops, moved, **options):
        return pl.pallas_call(
            body,
            cost_estimate=pl.CostEstimate(flops=flops, bytes_accessed=moved, transcendentals=0),
            compiler_params=pltpu.CompilerParams(vmem_limit_bytes=16 * 2**20),
            **options,
        )

    def along_row(piece, k):
        route = [(g, g // n_col * n_col + (g + k) % n_col) for g in range(n_group)]
        return lax.ppermute(piece, "group", route)

    def along_column(piece, k):
        route = [(g, (g // n_col + k) % n_row * n_col + g % n_col) for g in range(n_group)]
        return lax.ppermute(piece, "group", route)

    def to_block(piece, distance):
        return lax.ppermute(piece, "blk", [(i, (i + distance) % n_blk) for i in range(n_blk)])

    unit_shapes = (shape((rows, emb), F32), shape((rows, 1), F32), shape((rows, emb), BF16))
    txt_unit, txt_inv, txt_low = kernel(
        text_kernel,
        2 * rows * width * emb * 20,
        20 * width * (rows + emb),
        out_shape=unit_shapes,
        in_specs=[VMEM],
        out_specs=(VMEM,) * 3,
    )(text_emb)
    texts = [txt_low] + [along_column(txt_low, k) for k in range(1, n_row)]
    earlier_texts = [to_block(piece, 1) for piece in texts]

    img_unit, img_inv, img_low = kernel(
        project_kernel,
        2 * rows * width * emb,
        2 * width * (rows + emb),
        out_shape=unit_shapes,
        in_specs=[VMEM] * 2,
        out_specs=(VMEM,) * 3,
    )(img_feat, head_weight)

    images = [img_low] + [along_row(img_low, k) for k in range(1, n_col)]
    later_images = [to_block(piece, -1) for piece in images]

    def meetings(left, right, after):
        n_left = len(left)
        return kernel(
            functools.partial(meet_kernel, n_left),
            4 * n_left * len(right) * rows * rows * emb,
            2 * rows * emb * (2 * n_left + len(right)),
            out_shape=(shape((rows, emb), F32),) + (shape((rows, emb), BF16),) * (n_left - 1),
            in_specs=[VMEM] * 2 + [ANY] + [VMEM] * (n_left + len(right)),
            out_specs=(VMEM,) * n_left,
        )(natural_exponent_factor.reshape(1, 1), bias.reshape(1, 1), after, *left, *right)

    grad_img, *img_terms = meetings(images, texts + earlier_texts, bias)
    img_peers = [along_row(term, -k) for k, term in enumerate(img_terms, 1)]
    grad_txt, *txt_terms = meetings(texts, images + later_images, grad_img)
    txt_peers = [along_column(term, -k) for k, term in enumerate(txt_terms, 1)]

    d_feat, flag = kernel(
        feat_kernel,
        2 * rows * width * emb,
        4 * width * (rows + emb),
        out_shape=(shape((rows, width), F32), shape((8, 128), F32)),
        in_specs=[VMEM] * (4 + len(img_peers)),
        out_specs=(HBM, VMEM),
        scratch_shapes=[pltpu.VMEM((rows, width), F32), pltpu.SemaphoreType.DMA((parts,))],
    )(grad_img, img_unit, img_inv, head_weight, *img_peers)

    d_text = kernel(
        text_out_kernel,
        8 * rows * emb,
        12 * rows * emb,
        out_shape=shape((rows, emb), F32),
        in_specs=[ANY] + [VMEM] * (3 + len(txt_peers)),
        out_specs=VMEM,
    )(flag, grad_txt, txt_unit, txt_inv, *txt_peers)
    return d_feat, d_text


def solution(mesh):
    return jax.shard_map(
        body,
        mesh=mesh,
        in_specs=(P(("blk", "group"), None), P(), P(("blk", "group"), None), P(), P()),
        out_specs=(P(("blk", "group"), None), P(("blk", "group"), None)),
        check_vma=False,
    )
```

```python
import functools
import math

import jax
import jax.numpy as jnp
from jax import lax
from jax.experimental import pallas as pl
from jax.experimental.pallas import tpu as pltpu
from jax.sharding import PartitionSpec as P

EPS = 1e-06
F32 = jnp.float32
BF16 = jnp.bfloat16
CONTRACT_LAST = (((1,), (1,)), ((), ()))
VMEM = pl.BlockSpec(memory_space=pltpu.VMEM)
SMEM = pl.BlockSpec(memory_space=pltpu.SMEM)
ANY = pl.BlockSpec(memory_space=pl.ANY)
HBM = pl.BlockSpec(memory_space=pltpu.HBM)


def to_unit(values):
    inverse = lax.rsqrt(jnp.sum(values * values, axis=-1, keepdims=True) + EPS)
    return values * inverse, inverse


def unit_back(grad_in, unit_rows, inverse):
    return (grad_in - unit_rows * jnp.sum(unit_rows * grad_in, axis=-1, keepdims=True)) * inverse


def project_kernel(after_ref, img_ref, head_ref, unit_ref, inv_ref, low_ref):
    projected = jnp.dot(img_ref[...], head_ref[...], preferred_element_type=F32)
    unit, inverse = to_unit(projected)
    unit_ref[...] = unit
    inv_ref[...] = inverse
    low_ref[...] = unit.astype(BF16)


def meet(scale, bias, left, right, rows):
    z = scale * lax.dot_general(left, right, CONTRACT_LAST, preferred_element_type=F32) + bias
    row_ids = lax.broadcasted_iota(jnp.int32, z.shape, 0)
    col_ids = lax.broadcasted_iota(jnp.int32, z.shape, 1)
    positive = jnp.where((row_ids == col_ids) & (row_ids < rows), 1.0, 0.0)
    weight = (1.0 / (1.0 + jnp.exp(-z)) - positive).astype(BF16)
    return scale * jnp.dot(weight, right, preferred_element_type=F32)


def text_low(ref):
    return to_unit(ref[...].astype(F32))[0].astype(BF16)


def meet_kernel(left_is_text, n_left, n_out, scalar_ref, after_ref, *refs):
    left_refs, refs = refs[:n_left], refs[n_left:]
    right_refs, (grad_ref, *out_refs) = refs[:-n_out], refs[-n_out:]
    rows = grad_ref.shape[0]
    plain = lambda ref: ref[...]
    read_left, read_right = (text_low, plain) if left_is_text else (plain, text_low)
    left = jnp.concatenate([read_left(ref) for ref in left_refs], axis=0)
    right = jnp.concatenate([read_right(ref) for ref in right_refs], axis=0)
    grad = meet(scalar_ref[0:1, 0:1], scalar_ref[1:2, 0:1], left, right, rows)
    grad_ref[...] = grad[:rows]
    for k, ref in enumerate(out_refs, 1):
        ref[...] = grad[k * rows : (k + 1) * rows].astype(BF16)


def feat_kernel(grad_ref, unit_ref, inv_ref, head_ref, *refs):
    peer_refs, (out_ref, flag_ref, out_here, sems) = refs[:-4], refs[-4:]
    parts = sems.shape[0]
    width = head_ref.shape[0] // parts
    grad = grad_ref[...]
    for ref in peer_refs:
        grad += ref[...].astype(F32)
    low = unit_back(grad, unit_ref[...], inv_ref[...]).astype(BF16)
    copies = []
    for i in range(parts):
        span = pl.ds(i * width, width)
        out_here[:, span] = lax.dot_general(low, head_ref[span], CONTRACT_LAST, preferred_element_type=F32)
        copy = pltpu.make_async_copy(out_here.at[:, span], out_ref.at[:, span], sems.at[i])
        copy.start()
        copies.append(copy)
    for copy in copies:
        copy.wait()
    flag_ref[...] = jnp.zeros_like(flag_ref)


def mark_kernel(*refs):
    refs[-1][...] = jnp.zeros_like(refs[-1])


def text_out_kernel(after_ref, grad_ref, text_ref, *refs):
    peer_refs, out_ref = refs[:-1], refs[-1]
    grad = grad_ref[...]
    for ref in peer_refs:
        grad += ref[...].astype(F32)
    unit, inverse = to_unit(text_ref[...].astype(F32))
    out_ref[...] = unit_back(grad, unit, inverse)


def body(img_feat, head_weight, text_emb, natural_exponent_factor, bias):
    rows, width = img_feat.shape
    emb = text_emb.shape[1]
    n_blk, n_group = lax.axis_size("blk"), lax.axis_size("group")
    n_col = next(k for k in range(math.isqrt(n_group), 0, -1) if n_group % k == 0)
    n_row = n_group // n_col
    shape = jax.ShapeDtypeStruct
    parts = 4 if width % 512 == 0 else 1

    def kernel(body, flops, moved, **options):
        return pl.pallas_call(
            body,
            cost_estimate=pl.CostEstimate(flops=flops, bytes_accessed=moved, transcendentals=0),
            compiler_params=pltpu.CompilerParams(vmem_limit_bytes=16 * 2**20),
            **options,
        )

    side = n_col if n_row == n_col else 0

    def route(image_side, distance, k):
        pairs = []
        for i in range(n_blk):
            j = (i + distance) % n_blk
            along_row = image_side if side == 0 or j % 2 == 0 else not image_side
            for g in range(n_group):
                r, c = g // n_col, g % n_col
                r, c = (r, (c + k) % n_col) if along_row else ((r + k) % n_row, c)
                pairs.append((i * n_group + g, j * n_group + r * n_col + c))
        return pairs

    def send(piece, image_side, distance, k):
        return lax.ppermute(piece, ("blk", "group"), route(image_side, distance, k))

    def marked(after):
        return kernel(
            mark_kernel,
            2 * rows * emb,
            4 * rows * emb,
            out_shape=shape((8, 128), F32),
            in_specs=[ANY] * len(after),
            out_specs=VMEM,
        )(*after)

    first = lax.broadcasted_iota(jnp.int32, (8, 128), 0) == 0
    scalars = jnp.where(first, jnp.exp(natural_exponent_factor[0]), bias[0])

    unit_shapes = (shape((rows, emb), F32), shape((rows, 1), F32), shape((rows, emb), BF16))
    early = kernel(
        mark_kernel, 40 * rows * width * emb, 20 * width * (rows + emb), out_shape=shape((8, 128), F32), out_specs=VMEM
    )()
    early = lax.ppermute(early, "blk", [(i, i ^ 1 if n_blk % 2 == 0 else i) for i in range(n_blk)])
    earlier_texts = [send(text_emb, False, 1, k) for k in range(n_row)]
    texts = [text_emb] + [send(text_emb, False, 0, k) for k in range(1, n_row)]

    img_unit, img_inv, img_low = kernel(
        project_kernel,
        2 * rows * width * emb,
        2 * width * (rows + emb),
        out_shape=unit_shapes,
        in_specs=[ANY] + [VMEM] * 2,
        out_specs=(VMEM,) * 3,
    )(early, img_feat, head_weight)

    images = [img_low] + [send(img_low, True, 0, k) for k in range(1, n_col)]
    later_images = [send(img_low, True, -1, k) for k in range(n_col)]

    def meetings(left, right, after, left_is_text):
        n_left = len(left)
        return kernel(
            functools.partial(meet_kernel, left_is_text, n_left, sum(p.shape[0] for p in left) // rows),
            4 * n_left * len(right) * rows * rows * emb,
            2 * rows * emb * (2 * n_left + len(right)),
            out_shape=(shape((rows, emb), F32),) + (shape((rows, emb), BF16),) * (sum(p.shape[0] for p in left) // rows - 1),
            in_specs=[VMEM, ANY] + [VMEM] * (n_left + len(right)),
            out_specs=(VMEM,) * (sum(p.shape[0] for p in left) // rows),
        )(scalars, after, *left, *right)

    grad_img, *img_terms = meetings(images, texts + earlier_texts, marked(earlier_texts), False)
    img_peers = [send(term, True, 0, -k) for k, term in enumerate(img_terms, 1)]
    grad_txt, *txt_terms = meetings(texts, images + later_images, grad_img, True)
    txt_peers = [send(term, False, 0, -k) for k, term in enumerate(txt_terms, 1)]

    d_feat, flag = kernel(
        feat_kernel,
        2 * rows * width * emb,
        4 * width * (rows + emb),
        out_shape=(shape((rows, width), F32), shape((8, 128), F32)),
        in_specs=[VMEM] * (4 + len(img_peers)),
        out_specs=(HBM, VMEM),
        scratch_shapes=[pltpu.VMEM((rows, width), F32), pltpu.SemaphoreType.DMA((parts,))],
    )(grad_img, img_unit, img_inv, head_weight, *img_peers)

    d_text = kernel(
        text_out_kernel,
        8 * rows * emb,
        12 * rows * emb,
        out_shape=shape((rows, emb), F32),
        in_specs=[ANY] + [VMEM] * (2 + len(txt_peers)),
        out_specs=VMEM,
    )(flag, grad_txt, text_emb, *txt_peers)
    return d_feat, d_text


def solution(mesh):
    return jax.shard_map(
        body,
        mesh=mesh,
        in_specs=(P(("blk", "group"), None), P(), P(("blk", "group"), None), P(), P()),
        out_specs=(P(("blk", "group"), None), P(("blk", "group"), None)),
        check_vma=False,
    )
```

```python
import functools
import math

import jax
import jax.numpy as jnp
from jax import lax
from jax.experimental import pallas as pl
from jax.experimental.pallas import tpu as pltpu
from jax.sharding import PartitionSpec as P

EPS = 1e-06
F32 = jnp.float32
BF16 = jnp.bfloat16
CONTRACT_LAST = (((1,), (1,)), ((), ()))
VMEM = pl.BlockSpec(memory_space=pltpu.VMEM)
SMEM = pl.BlockSpec(memory_space=pltpu.SMEM)
ANY = pl.BlockSpec(memory_space=pl.ANY)
HBM = pl.BlockSpec(memory_space=pltpu.HBM)


def to_unit(values):
    inverse = lax.rsqrt(jnp.sum(values * values, axis=-1, keepdims=True) + EPS)
    return values * inverse, inverse


def unit_back(grad_in, unit_rows, inverse):
    return (grad_in - unit_rows * jnp.sum(unit_rows * grad_in, axis=-1, keepdims=True)) * inverse


def project_kernel(after_ref, img_ref, head_ref, unit_ref, inv_ref, low_ref):
    projected = jnp.dot(img_ref[...], head_ref[...], preferred_element_type=F32)
    unit, inverse = to_unit(projected)
    unit_ref[...] = unit
    inv_ref[...] = inverse
    low_ref[...] = unit.astype(BF16)


def meet(scale, bias, left, right, rows):
    z = scale * lax.dot_general(left, right, CONTRACT_LAST, preferred_element_type=F32) + bias
    row_ids = lax.broadcasted_iota(jnp.int32, z.shape, 0)
    col_ids = lax.broadcasted_iota(jnp.int32, z.shape, 1)
    positive = jnp.where((row_ids == col_ids) & (row_ids < rows), 1.0, 0.0)
    weight = (1.0 / (1.0 + jnp.exp(-z)) - positive).astype(BF16)
    return scale * jnp.dot(weight, right, preferred_element_type=F32)


def scalar_kernel(factor_ref, bias_ref, *refs):
    first = lax.broadcasted_iota(jnp.int32, refs[-1].shape, 0) == 0
    refs[-1][...] = jnp.where(first, jnp.exp(jnp.full(refs[-1].shape, factor_ref[0], F32)), bias_ref[0])


def text_low(ref):
    return to_unit(ref[...].astype(F32))[0].astype(BF16)


def meet_kernel(left_is_text, n_left, n_out, scalar_ref, after_ref, *refs):
    left_refs, refs = refs[:n_left], refs[n_left:]
    right_refs, (grad_ref, *out_refs) = refs[:-n_out], refs[-n_out:]
    rows = grad_ref.shape[0]
    plain = lambda ref: ref[...]
    read_left, read_right = (text_low, plain) if left_is_text else (plain, text_low)
    left = jnp.concatenate([read_left(ref) for ref in left_refs], axis=0)
    right = jnp.concatenate([read_right(ref) for ref in right_refs], axis=0)
    grad = meet(scalar_ref[0:1, 0:1], scalar_ref[1:2, 0:1], left, right, rows)
    grad_ref[...] = grad[:rows]
    for k, ref in enumerate(out_refs, 1):
        ref[...] = grad[k * rows : (k + 1) * rows].astype(BF16)


def feat_kernel(grad_ref, unit_ref, inv_ref, head_ref, *refs):
    peer_refs, (out_ref, flag_ref, out_here, sems) = refs[:-4], refs[-4:]
    parts = sems.shape[0]
    width = head_ref.shape[0] // parts
    grad = grad_ref[...]
    for ref in peer_refs:
        grad += ref[...].astype(F32)
    low = unit_back(grad, unit_ref[...], inv_ref[...]).astype(BF16)
    copies = []
    for i in range(parts):
        span = pl.ds(i * width, width)
        out_here[:, span] = lax.dot_general(low, head_ref[span], CONTRACT_LAST, preferred_element_type=F32)
        copy = pltpu.make_async_copy(out_here.at[:, span], out_ref.at[:, span], sems.at[i])
        copy.start()
        copies.append(copy)
    for copy in copies:
        copy.wait()
    flag_ref[...] = jnp.zeros_like(flag_ref)


def mark_kernel(*refs):
    refs[-1][...] = jnp.zeros_like(refs[-1])


def text_out_kernel(after_ref, grad_ref, text_ref, *refs):
    peer_refs, out_ref = refs[:-1], refs[-1]
    grad = grad_ref[...]
    for ref in peer_refs:
        grad += ref[...].astype(F32)
    unit, inverse = to_unit(text_ref[...].astype(F32))
    out_ref[...] = unit_back(grad, unit, inverse)


def body(img_feat, head_weight, text_emb, natural_exponent_factor, bias):
    rows, width = img_feat.shape
    emb = text_emb.shape[1]
    n_blk, n_group = lax.axis_size("blk"), lax.axis_size("group")
    n_col = next(k for k in range(math.isqrt(n_group), 0, -1) if n_group % k == 0)
    n_row = n_group // n_col
    shape = jax.ShapeDtypeStruct
    parts = 4 if width % 512 == 0 else 1

    def kernel(body, flops, moved, **options):
        return pl.pallas_call(
            body,
            cost_estimate=pl.CostEstimate(flops=flops, bytes_accessed=moved, transcendentals=0),
            compiler_params=pltpu.CompilerParams(vmem_limit_bytes=16 * 2**20),
            **options,
        )

    side = n_col if n_row == n_col else 0

    def route(image_side, distance, k):
        pairs = []
        for i in range(n_blk):
            j = (i + distance) % n_blk
            along_row = image_side if side == 0 or j % 2 == 0 else not image_side
            for g in range(n_group):
                r, c = g // n_col, g % n_col
                r, c = (r, (c + k) % n_col) if along_row else ((r + k) % n_row, c)
                pairs.append((i * n_group + g, j * n_group + r * n_col + c))
        return pairs

    def send(piece, image_side, distance, k):
        return lax.ppermute(piece, ("blk", "group"), route(image_side, distance, k))

    def marked(after):
        return kernel(
            mark_kernel,
            2 * rows * emb,
            4 * rows * emb,
            out_shape=shape((8, 128), F32),
            in_specs=[ANY] * len(after),
            out_specs=VMEM,
        )(*after)


    unit_shapes = (shape((rows, emb), F32), shape((rows, 1), F32), shape((rows, emb), BF16))
    early = kernel(
        mark_kernel, 40 * rows * width * emb, 20 * width * (rows + emb), out_shape=shape((8, 128), F32), out_specs=VMEM
    )()
    early = lax.ppermute(early, "blk", [(i, i ^ 1 if n_blk % 2 == 0 else i) for i in range(n_blk)])
    earlier_texts = [send(text_emb, False, 1, k) for k in range(n_row)]
    texts = [text_emb] + [send(text_emb, False, 0, k) for k in range(1, n_row)]

    img_unit, img_inv, img_low = kernel(
        project_kernel,
        2 * rows * width * emb,
        2 * width * (rows + emb),
        out_shape=unit_shapes,
        in_specs=[ANY] + [VMEM] * 2,
        out_specs=(VMEM,) * 3,
    )(early, img_feat, head_weight)

    images = [img_low] + [send(img_low, True, 0, k) for k in range(1, n_col)]
    later_images = [send(img_low, True, -1, k) for k in range(n_col)]

    def meetings(left, right, after, left_is_text):
        n_left = len(left)
        return kernel(
            functools.partial(meet_kernel, left_is_text, n_left, sum(p.shape[0] for p in left) // rows),
            4 * n_left * len(right) * rows * rows * emb,
            2 * rows * emb * (2 * n_left + len(right)),
            out_shape=(shape((rows, emb), F32),) + (shape((rows, emb), BF16),) * (sum(p.shape[0] for p in left) // rows - 1),
            in_specs=[VMEM, ANY] + [VMEM] * (n_left + len(right)),
            out_specs=(VMEM,) * (sum(p.shape[0] for p in left) // rows),
        )(scalars, after, *left, *right)

    arrived = earlier_texts
    scalars = kernel(
        scalar_kernel,
        0,
        0,
        out_shape=shape((8, 128), F32),
        in_specs=[SMEM] * 2 + [ANY] * len(arrived),
        out_specs=VMEM,
    )(natural_exponent_factor, bias, *arrived)
    grad_img, *img_terms = meetings(images, texts + earlier_texts, scalars, False)
    img_peers = [send(term, True, 0, -k) for k, term in enumerate(img_terms, 1)]
    grad_txt, *txt_terms = meetings(texts, images + later_images, grad_img, True)
    txt_peers = [send(term, False, 0, -k) for k, term in enumerate(txt_terms, 1)]

    d_feat, flag = kernel(
        feat_kernel,
        2 * rows * width * emb,
        4 * width * (rows + emb),
        out_shape=(shape((rows, width), F32), shape((8, 128), F32)),
        in_specs=[VMEM] * (4 + len(img_peers)),
        out_specs=(HBM, VMEM),
        scratch_shapes=[pltpu.VMEM((rows, width), F32), pltpu.SemaphoreType.DMA((parts,))],
    )(grad_img, img_unit, img_inv, head_weight, *img_peers)

    d_text = kernel(
        text_out_kernel,
        8 * rows * emb,
        12 * rows * emb,
        out_shape=shape((rows, emb), F32),
        in_specs=[ANY] + [VMEM] * (2 + len(txt_peers)),
        out_specs=VMEM,
    )(flag, grad_txt, text_emb, *txt_peers)
    return d_feat, d_text


def solution(mesh):
    return jax.shard_map(
        body,
        mesh=mesh,
        in_specs=(P(("blk", "group"), None), P(), P(("blk", "group"), None), P(), P()),
        out_specs=(P(("blk", "group"), None), P(("blk", "group"), None)),
        check_vma=False,
    )
```

```python
import functools
import math

import jax
import jax.numpy as jnp
from jax import lax
from jax.experimental import pallas as pl
from jax.experimental.pallas import tpu as pltpu
from jax.sharding import PartitionSpec as P

EPS = 1e-06
LOG2_E = math.log2(math.e)
F32 = jnp.float32
BF16 = jnp.bfloat16
CONTRACT_LAST = (((1,), (1,)), ((), ()))
VMEM = pl.BlockSpec(memory_space=pltpu.VMEM)
ANY = pl.BlockSpec(memory_space=pl.ANY)
HBM = pl.BlockSpec(memory_space=pltpu.HBM)


def to_unit(values):
    inverse = lax.rsqrt(jnp.sum(values * values, axis=-1, keepdims=True) + EPS)
    return values * inverse, inverse


def unit_back(grad_in, unit_rows, inverse):
    return (grad_in - unit_rows * jnp.sum(unit_rows * grad_in, axis=-1, keepdims=True)) * inverse


def project_kernel(after_ref, img_ref, head_ref, unit_ref, inv_ref, low_ref):
    projected = jnp.dot(img_ref[...], head_ref[...], preferred_element_type=F32)
    unit, inverse = to_unit(projected)
    unit_ref[...] = unit
    inv_ref[...] = inverse
    low_ref[...] = unit.astype(BF16)


def text_low(ref):
    return to_unit(ref[...].astype(F32))[0].astype(BF16)


def low_kernel(text_ref, after_ref, low_ref):
    low_ref[...] = text_low(text_ref)


def meet(scalar_ref, left, right, weight_ref, grad_ref, term_refs):
    rows = grad_ref.shape[0]
    scale, bias = scalar_ref[0:1, 0:1], scalar_ref[1:2, 0:1]
    similarity = lax.dot_general(left, right, CONTRACT_LAST, preferred_element_type=F32)
    power = jnp.exp2(similarity * (scale * -LOG2_E) + bias * -LOG2_E)
    sigmoid = 1.0 / (1.0 + power)
    weight_ref[...] = sigmoid.astype(BF16)
    row_ids = lax.broadcasted_iota(jnp.int32, (rows, rows), 0)
    col_ids = lax.broadcasted_iota(jnp.int32, (rows, rows), 1)
    own = sigmoid[:rows, :rows]
    weight_ref[:rows, :rows] = jnp.where(row_ids == col_ids, own - 1.0, own).astype(BF16)
    grad = scale * jnp.dot(weight_ref[...], right, preferred_element_type=F32)
    grad_ref[...] = grad[:rows]
    for k, ref in enumerate(term_refs, 1):
        ref[...] = grad[k * rows : (k + 1) * rows].astype(BF16)


def image_kernel(n_col, n_row, scalar_ref, *refs):
    refs = refs[n_row:]
    image_refs, refs = refs[:n_col], refs[n_col:]
    raw_refs, refs = refs[:n_row], refs[n_row:]
    earlier_refs, refs = refs[:n_row], refs[n_row:]
    (grad_ref, *term_refs), weight_ref = refs[:-1], refs[-1]
    images = jnp.concatenate([ref[...] for ref in image_refs], axis=0)
    texts = jnp.concatenate([text_low(ref) for ref in raw_refs] + [ref[...] for ref in earlier_refs], axis=0)
    meet(scalar_ref, images, texts, weight_ref, grad_ref, term_refs)


def text_kernel(n_row, n_image, scalar_ref, after_ref, *refs):
    text_refs, refs = refs[:n_row], refs[n_row:]
    image_refs, refs = refs[:n_image], refs[n_image:]
    (grad_ref, *term_refs), weight_ref = refs[:-1], refs[-1]
    texts = jnp.concatenate([text_low(ref) for ref in text_refs], axis=0)
    images = jnp.concatenate([ref[...] for ref in image_refs], axis=0)
    meet(scalar_ref, texts, images, weight_ref, grad_ref, term_refs)


def feat_kernel(grad_ref, unit_ref, inv_ref, head_ref, text_ref, *refs):
    peer_refs, (out_ref, text_unit_ref, text_inv_ref, out_here, sems) = refs[:-5], refs[-5:]
    parts = sems.shape[0]
    width = head_ref.shape[0] // parts
    grad = grad_ref[...]
    for ref in peer_refs:
        grad += ref[...].astype(F32)
    low = unit_back(grad, unit_ref[...], inv_ref[...]).astype(BF16)
    copies = []
    for i in range(parts):
        span = pl.ds(i * width, width)
        out_here[:, span] = lax.dot_general(low, head_ref[span], CONTRACT_LAST, preferred_element_type=F32)
        copy = pltpu.make_async_copy(out_here.at[:, span], out_ref.at[:, span], sems.at[i])
        copy.start()
        copies.append(copy)
    text_unit_ref[...], text_inv_ref[...] = to_unit(text_ref[...].astype(F32))
    for copy in copies:
        copy.wait()


def mark_kernel(out_ref):
    out_ref[...] = jnp.zeros_like(out_ref)


def text_out_kernel(grad_ref, unit_ref, inv_ref, *refs):
    peer_refs, out_ref = refs[:-1], refs[-1]
    grad = grad_ref[...]
    for ref in peer_refs:
        grad += ref[...].astype(F32)
    out_ref[...] = unit_back(grad, unit_ref[...], inv_ref[...])


def body(img_feat, head_weight, text_emb, natural_exponent_factor, bias):
    rows, width = img_feat.shape
    emb = text_emb.shape[1]
    n_blk, n_group = lax.axis_size("blk"), lax.axis_size("group")
    n_col = next(k for k in range(math.isqrt(n_group), 0, -1) if n_group % k == 0)
    n_row = n_group // n_col
    shape = jax.ShapeDtypeStruct
    parts = 8 if width % 1024 == 0 else 1

    def kernel(body, flops, moved, **options):
        return pl.pallas_call(
            body,
            cost_estimate=pl.CostEstimate(flops=flops, bytes_accessed=moved, transcendentals=0),
            compiler_params=pltpu.CompilerParams(vmem_limit_bytes=16 * 2**20),
            **options,
        )

    side = n_col if n_row == n_col else 0

    def route(image_side, distance, k):
        pairs = []
        for i in range(n_blk):
            j = (i + distance) % n_blk
            along_row = image_side if side == 0 or j % 2 == 1 else not image_side
            for g in range(n_group):
                r, c = g // n_col, g % n_col
                r, c = (r, (c + k) % n_col) if along_row else ((r + k) % n_row, c)
                pairs.append((i * n_group + g, j * n_group + r * n_col + c))
        return pairs

    def send(piece, image_side, distance, k):
        return lax.ppermute(piece, ("blk", "group"), route(image_side, distance, k))

    first = lax.broadcasted_iota(jnp.int32, (8, 128), 0) == 0
    scalars = jnp.where(first, jnp.exp(natural_exponent_factor[0]), bias[0])

    unit_shapes = (shape((rows, emb), F32), shape((rows, 1), F32), shape((rows, emb), BF16))
    early = kernel(
        mark_kernel, 40 * rows * width * emb, 20 * width * (rows + emb), out_shape=shape((8, 128), F32), out_specs=VMEM
    )()
    earlier_texts = [send(text_emb, False, 1, k) for k in range(n_row)]
    texts = [text_emb] + [send(text_emb, False, 0, k) for k in range(1, n_row)]

    img_unit, img_inv, img_low = kernel(
        project_kernel,
        2 * rows * width * emb,
        2 * width * (rows + emb),
        out_shape=unit_shapes,
        in_specs=[ANY] + [VMEM] * 2,
        out_specs=(VMEM,) * 3,
    )(early, img_feat, head_weight)

    images = [img_low] + [send(img_low, True, 0, k) for k in range(1, n_col)]
    later_images = [send(img_low, True, -1, k) for k in range(n_col)]

    low_piece, grad_piece = shape((rows, emb), BF16), shape((rows, emb), F32)
    earlier_lows, after = [], scalars
    for piece in earlier_texts:
        after = kernel(
            low_kernel,
            8 * rows * emb,
            4 * rows * emb,
            out_shape=low_piece,
            in_specs=[VMEM, ANY],
            out_specs=VMEM,
        )(piece, after)
        earlier_lows.append(after)

    grad_img, *img_terms = kernel(
        functools.partial(image_kernel, n_col, n_row),
        8 * n_col * n_row * rows * rows * emb,
        2 * rows * emb * (2 * n_col + 3 * n_row),
        out_shape=(grad_piece,) + (low_piece,) * (n_col - 1),
        in_specs=[VMEM] + [ANY] * n_row + [VMEM] * (n_col + 2 * n_row),
        out_specs=(VMEM,) * n_col,
        scratch_shapes=[pltpu.VMEM((n_col * rows, 2 * n_row * rows), BF16)],
    )(scalars, *earlier_texts, *images, *texts, *earlier_lows)
    img_peers = [send(term, True, 0, -k) for k, term in enumerate(img_terms, 1)]

    grad_txt, *txt_terms = kernel(
        functools.partial(text_kernel, n_row, 2 * n_col),
        8 * n_col * n_row * rows * rows * emb,
        2 * rows * emb * (2 * n_col + 3 * n_row),
        out_shape=(grad_piece,) + (low_piece,) * (n_row - 1),
        in_specs=[VMEM, ANY] + [VMEM] * (n_row + 2 * n_col),
        out_specs=(VMEM,) * n_row,
        scratch_shapes=[pltpu.VMEM((n_row * rows, 2 * n_col * rows), BF16)],
    )(scalars, grad_img, *texts, *images, *later_images)
    txt_peers = [send(term, False, 0, -k) for k, term in enumerate(txt_terms, 1)]

    d_feat, txt_unit, txt_inv = kernel(
        feat_kernel,
        2 * rows * width * emb,
        4 * width * (rows + emb),
        out_shape=(shape((rows, width), F32), grad_piece, shape((rows, 1), F32)),
        in_specs=[VMEM] * (5 + len(img_peers)),
        out_specs=(HBM, VMEM, VMEM),
        scratch_shapes=[pltpu.VMEM((rows, width), F32), pltpu.SemaphoreType.DMA((parts,))],
    )(grad_img, img_unit, img_inv, head_weight, text_emb, *img_peers)

    d_text = kernel(
        text_out_kernel,
        8 * rows * emb,
        12 * rows * emb,
        out_shape=shape((rows, emb), F32),
        in_specs=[VMEM] * (3 + len(txt_peers)),
        out_specs=VMEM,
    )(grad_txt, txt_unit, txt_inv, *txt_peers)
    return d_feat, d_text


def solution(mesh):
    return jax.shard_map(
        body,
        mesh=mesh,
        in_specs=(P(("blk", "group"), None), P(), P(("blk", "group"), None), P(), P()),
        out_specs=(P(("blk", "group"), None), P(("blk", "group"), None)),
        check_vma=False,
    )
```

```python
import functools
import math

import jax
import jax.numpy as jnp
from jax import lax
from jax.experimental import pallas as pl
from jax.experimental.pallas import tpu as pltpu
from jax.sharding import PartitionSpec as P

EPS = 1e-06
LOG2_E = math.log2(math.e)
F32 = jnp.float32
BF16 = jnp.bfloat16
CONTRACT_LAST = (((1,), (1,)), ((), ()))
VMEM = pl.BlockSpec(memory_space=pltpu.VMEM)
ANY = pl.BlockSpec(memory_space=pl.ANY)
HBM = pl.BlockSpec(memory_space=pltpu.HBM)


def to_unit(values):
    inverse = lax.rsqrt(jnp.sum(values * values, axis=-1, keepdims=True) + EPS)
    return values * inverse, inverse


def unit_back(grad_in, unit_rows, inverse):
    return (grad_in - unit_rows * jnp.sum(unit_rows * grad_in, axis=-1, keepdims=True)) * inverse


def project_kernel(after_ref, img_ref, head_ref, unit_ref, inv_ref, low_ref):
    projected = jnp.dot(img_ref[...], head_ref[...], preferred_element_type=F32)
    unit, inverse = to_unit(projected)
    unit_ref[...] = unit
    inv_ref[...] = inverse
    low_ref[...] = unit.astype(BF16)


def text_low(ref):
    return to_unit(ref[...].astype(F32))[0].astype(BF16)


def low_kernel(text_ref, after_ref, low_ref):
    low_ref[...] = text_low(text_ref)


def meet(scalar_ref, left, right, weight_ref, grad_ref, term_refs):
    rows = grad_ref.shape[0]
    scale, bias = scalar_ref[0:1, 0:1], scalar_ref[1:2, 0:1]
    similarity = lax.dot_general(left, right, CONTRACT_LAST, preferred_element_type=F32)
    power = jnp.exp2(similarity * (scale * -LOG2_E) + bias * -LOG2_E)
    sigmoid = 1.0 / (1.0 + power)
    weight_ref[...] = sigmoid.astype(BF16)
    row_ids = lax.broadcasted_iota(jnp.int32, (rows, rows), 0)
    col_ids = lax.broadcasted_iota(jnp.int32, (rows, rows), 1)
    own = sigmoid[:rows, :rows]
    weight_ref[:rows, :rows] = jnp.where(row_ids == col_ids, own - 1.0, own).astype(BF16)
    grad = scale * jnp.dot(weight_ref[...], right, preferred_element_type=F32)
    grad_ref[...] = grad[:rows]
    for k, ref in enumerate(term_refs, 1):
        ref[...] = grad[k * rows : (k + 1) * rows].astype(BF16)


def image_kernel(n_col, n_row, scalar_ref, *refs):
    refs = refs[n_row:]
    image_refs, refs = refs[:n_col], refs[n_col:]
    raw_refs, refs = refs[:n_row], refs[n_row:]
    earlier_refs, refs = refs[:n_row], refs[n_row:]
    (grad_ref, *term_refs), weight_ref = refs[:-1], refs[-1]
    images = jnp.concatenate([ref[...] for ref in image_refs], axis=0)
    texts = jnp.concatenate([text_low(ref) for ref in raw_refs] + [ref[...] for ref in earlier_refs], axis=0)
    meet(scalar_ref, images, texts, weight_ref, grad_ref, term_refs)


def text_kernel(n_row, n_image, scalar_ref, after_ref, *refs):
    text_refs, refs = refs[:n_row], refs[n_row:]
    image_refs, refs = refs[:n_image], refs[n_image:]
    (grad_ref, *term_refs), weight_ref = refs[:-1], refs[-1]
    texts = jnp.concatenate([text_low(ref) for ref in text_refs], axis=0)
    images = jnp.concatenate([ref[...] for ref in image_refs], axis=0)
    meet(scalar_ref, texts, images, weight_ref, grad_ref, term_refs)


def feat_kernel(grad_ref, unit_ref, inv_ref, head_ref, text_ref, *refs):
    peer_refs, (out_ref, text_unit_ref, text_inv_ref, out_here, sems) = refs[:-5], refs[-5:]
    parts = sems.shape[0]
    width = head_ref.shape[0] // parts
    grad = grad_ref[...]
    for ref in peer_refs:
        grad += ref[...].astype(F32)
    low = unit_back(grad, unit_ref[...], inv_ref[...]).astype(BF16)
    copies = []
    for i in range(parts):
        span = pl.ds(i * width, width)
        out_here[:, span] = lax.dot_general(low, head_ref[span], CONTRACT_LAST, preferred_element_type=F32)
        copy = pltpu.make_async_copy(out_here.at[:, span], out_ref.at[:, span], sems.at[i])
        copy.start()
        copies.append(copy)
    text_unit_ref[...], text_inv_ref[...] = to_unit(text_ref[...].astype(F32))
    for copy in copies:
        copy.wait()


def mark_kernel(out_ref):
    out_ref[...] = jnp.zeros_like(out_ref)


def text_out_kernel(grad_ref, unit_ref, inv_ref, *refs):
    peer_refs, out_ref = refs[:-1], refs[-1]
    grad = grad_ref[...]
    for ref in peer_refs:
        grad += ref[...].astype(F32)
    out_ref[...] = unit_back(grad, unit_ref[...], inv_ref[...])


def body(img_feat, head_weight, text_emb, natural_exponent_factor, bias):
    rows, width = img_feat.shape
    emb = text_emb.shape[1]
    n_blk, n_group = lax.axis_size("blk"), lax.axis_size("group")
    n_col = next(k for k in range(math.isqrt(n_group), 0, -1) if n_group % k == 0)
    n_row = n_group // n_col
    shape = jax.ShapeDtypeStruct
    parts = 12 if width % 1536 == 0 else 1

    def kernel(body, flops, moved, **options):
        return pl.pallas_call(
            body,
            cost_estimate=pl.CostEstimate(flops=flops, bytes_accessed=moved, transcendentals=0),
            compiler_params=pltpu.CompilerParams(vmem_limit_bytes=16 * 2**20),
            **options,
        )

    side = n_col if n_row == n_col else 0

    def route(image_side, distance, k):
        pairs = []
        for i in range(n_blk):
            j = (i + distance) % n_blk
            along_row = image_side if side == 0 or j % 2 == 1 else not image_side
            for g in range(n_group):
                r, c = g // n_col, g % n_col
                r, c = (r, (c + k) % n_col) if along_row else ((r + k) % n_row, c)
                pairs.append((i * n_group + g, j * n_group + r * n_col + c))
        return pairs

    def send(piece, image_side, distance, k):
        return lax.ppermute(piece, ("blk", "group"), route(image_side, distance, k))

    first = lax.broadcasted_iota(jnp.int32, (8, 128), 0) == 0
    scalars = jnp.where(first, jnp.exp(natural_exponent_factor[0]), bias[0])

    unit_shapes = (shape((rows, emb), F32), shape((rows, 1), F32), shape((rows, emb), BF16))
    early = kernel(
        mark_kernel, 40 * rows * width * emb, 20 * width * (rows + emb), out_shape=shape((8, 128), F32), out_specs=VMEM
    )()
    earlier_texts = [send(text_emb, False, 1, k) for k in range(n_row)]
    texts = [text_emb] + [send(text_emb, False, 0, k) for k in range(1, n_row)]

    img_unit, img_inv, img_low = kernel(
        project_kernel,
        2 * rows * width * emb,
        2 * width * (rows + emb),
        out_shape=unit_shapes,
        in_specs=[ANY] + [VMEM] * 2,
        out_specs=(VMEM,) * 3,
    )(early, img_feat, head_weight)

    images = [img_low] + [send(img_low, True, 0, k) for k in range(1, n_col)]
    later_images = [send(img_low, True, -1, k) for k in range(n_col)]

    low_piece, grad_piece = shape((rows, emb), BF16), shape((rows, emb), F32)
    earlier_lows, after = [], scalars
    for piece in earlier_texts:
        after = kernel(
            low_kernel,
            8 * rows * emb,
            4 * rows * emb,
            out_shape=low_piece,
            in_specs=[VMEM, ANY],
            out_specs=VMEM,
        )(piece, after)
        earlier_lows.append(after)

    grad_img, *img_terms = kernel(
        functools.partial(image_kernel, n_col, n_row),
        8 * n_col * n_row * rows * rows * emb,
        2 * rows * emb * (2 * n_col + 3 * n_row),
        out_shape=(grad_piece,) + (low_piece,) * (n_col - 1),
        in_specs=[VMEM] + [ANY] * n_row + [VMEM] * (n_col + 2 * n_row),
        out_specs=(VMEM,) * n_col,
        scratch_shapes=[pltpu.VMEM((n_col * rows, 2 * n_row * rows), BF16)],
    )(scalars, *earlier_texts, *images, *texts, *earlier_lows)
    img_peers = [send(term, True, 0, -k) for k, term in enumerate(img_terms, 1)]

    grad_txt, *txt_terms = kernel(
        functools.partial(text_kernel, n_row, 2 * n_col),
        8 * n_col * n_row * rows * rows * emb,
        2 * rows * emb * (2 * n_col + 3 * n_row),
        out_shape=(grad_piece,) + (low_piece,) * (n_row - 1),
        in_specs=[VMEM, ANY] + [VMEM] * (n_row + 2 * n_col),
        out_specs=(VMEM,) * n_row,
        scratch_shapes=[pltpu.VMEM((n_row * rows, 2 * n_col * rows), BF16)],
    )(scalars, grad_img, *texts, *images, *later_images)
    txt_peers = [send(term, False, 0, -k) for k, term in enumerate(txt_terms, 1)]

    d_feat, txt_unit, txt_inv = kernel(
        feat_kernel,
        2 * rows * width * emb,
        4 * width * (rows + emb),
        out_shape=(shape((rows, width), F32), grad_piece, shape((rows, 1), F32)),
        in_specs=[VMEM] * (5 + len(img_peers)),
        out_specs=(HBM, VMEM, VMEM),
        scratch_shapes=[pltpu.VMEM((rows, width), F32), pltpu.SemaphoreType.DMA((parts,))],
    )(grad_img, img_unit, img_inv, head_weight, text_emb, *img_peers)

    d_text = kernel(
        text_out_kernel,
        8 * rows * emb,
        12 * rows * emb,
        out_shape=shape((rows, emb), F32),
        in_specs=[VMEM] * (3 + len(txt_peers)),
        out_specs=VMEM,
    )(grad_txt, txt_unit, txt_inv, *txt_peers)
    return d_feat, d_text


def solution(mesh):
    return jax.shard_map(
        body,
        mesh=mesh,
        in_specs=(P(("blk", "group"), None), P(), P(("blk", "group"), None), P(), P()),
        out_specs=(P(("blk", "group"), None), P(("blk", "group"), None)),
        check_vma=False,
    )
```

```python
import functools
import math

import jax
import jax.numpy as jnp
from jax import lax
from jax.experimental import pallas as pl
from jax.experimental.pallas import tpu as pltpu
from jax.sharding import PartitionSpec as P

EPS = 1e-06
LOG2_E = math.log2(math.e)
F32 = jnp.float32
BF16 = jnp.bfloat16
CONTRACT_LAST = (((1,), (1,)), ((), ()))
VMEM = pl.BlockSpec(memory_space=pltpu.VMEM)
ANY = pl.BlockSpec(memory_space=pl.ANY)
HBM = pl.BlockSpec(memory_space=pltpu.HBM)


def to_unit(values):
    inverse = lax.rsqrt(jnp.sum(values * values, axis=-1, keepdims=True) + EPS)
    return values * inverse, inverse


def unit_back(grad_in, unit_rows, inverse):
    return (grad_in - unit_rows * jnp.sum(unit_rows * grad_in, axis=-1, keepdims=True)) * inverse


def project_kernel(after_ref, img_ref, head_ref, unit_ref, inv_ref, low_ref):
    projected = jnp.dot(img_ref[...], head_ref[...], preferred_element_type=F32)
    unit, inverse = to_unit(projected)
    unit_ref[...] = unit
    inv_ref[...] = inverse
    low_ref[...] = unit.astype(BF16)


def text_low(ref):
    return to_unit(ref[...].astype(F32))[0].astype(BF16)


def low_kernel(text_ref, after_ref, low_ref):
    low_ref[...] = text_low(text_ref)


def meet(scalar_ref, left, right, weight_ref, grad_ref, term_refs):
    rows = grad_ref.shape[0]
    scale, bias = scalar_ref[0:1, 0:1], scalar_ref[1:2, 0:1]
    similarity = lax.dot_general(left, right, CONTRACT_LAST, preferred_element_type=F32)
    power = jnp.exp2(similarity * (scale * -LOG2_E) + bias * -LOG2_E)
    sigmoid = 1.0 / (1.0 + power)
    weight_ref[...] = sigmoid.astype(BF16)
    row_ids = lax.broadcasted_iota(jnp.int32, (rows, rows), 0)
    col_ids = lax.broadcasted_iota(jnp.int32, (rows, rows), 1)
    own = sigmoid[:rows, :rows]
    weight_ref[:rows, :rows] = jnp.where(row_ids == col_ids, own - 1.0, own).astype(BF16)
    grad = scale * jnp.dot(weight_ref[...], right, preferred_element_type=F32)
    grad_ref[...] = grad[:rows]
    for k, ref in enumerate(term_refs, 1):
        ref[...] = grad[k * rows : (k + 1) * rows].astype(BF16)


def image_kernel(n_col, n_row, scalar_ref, *refs):
    refs = refs[n_row:]
    image_refs, refs = refs[:n_col], refs[n_col:]
    raw_refs, refs = refs[:n_row], refs[n_row:]
    earlier_refs, refs = refs[:n_row], refs[n_row:]
    (grad_ref, *term_refs), weight_ref = refs[:-1], refs[-1]
    images = jnp.concatenate([ref[...] for ref in image_refs], axis=0)
    texts = jnp.concatenate([text_low(ref) for ref in raw_refs] + [ref[...] for ref in earlier_refs], axis=0)
    meet(scalar_ref, images, texts, weight_ref, grad_ref, term_refs)


def text_kernel(n_row, n_image, scalar_ref, *refs):
    text_refs, refs = refs[:n_row], refs[n_row:]
    image_refs, refs = refs[:n_image], refs[n_image:]
    (grad_ref, *term_refs), weight_ref = refs[:-1], refs[-1]
    texts = jnp.concatenate([text_low(ref) for ref in text_refs], axis=0)
    images = jnp.concatenate([ref[...] for ref in image_refs], axis=0)
    meet(scalar_ref, texts, images, weight_ref, grad_ref, term_refs)


def feat_kernel(grad_ref, unit_ref, inv_ref, head_ref, text_ref, *refs):
    peer_refs, (out_ref, text_unit_ref, text_inv_ref, out_here, sems) = refs[:-5], refs[-5:]
    parts = sems.shape[0]
    width = head_ref.shape[0] // parts
    grad = grad_ref[...]
    for ref in peer_refs:
        grad += ref[...].astype(F32)
    low = unit_back(grad, unit_ref[...], inv_ref[...]).astype(BF16)
    copies = []
    for i in range(parts):
        span = pl.ds(i * width, width)
        out_here[:, span] = lax.dot_general(low, head_ref[span], CONTRACT_LAST, preferred_element_type=F32)
        copy = pltpu.make_async_copy(out_here.at[:, span], out_ref.at[:, span], sems.at[i])
        copy.start()
        copies.append(copy)
    text_unit_ref[...], text_inv_ref[...] = to_unit(text_ref[...].astype(F32))
    for copy in copies:
        copy.wait()


def mark_kernel(out_ref):
    out_ref[...] = jnp.zeros_like(out_ref)


def text_out_kernel(grad_ref, unit_ref, inv_ref, *refs):
    peer_refs, out_ref = refs[:-1], refs[-1]
    grad = grad_ref[...]
    for ref in peer_refs:
        grad += ref[...].astype(F32)
    out_ref[...] = unit_back(grad, unit_ref[...], inv_ref[...])


def body(img_feat, head_weight, text_emb, natural_exponent_factor, bias):
    rows, width = img_feat.shape
    emb = text_emb.shape[1]
    n_blk, n_group = lax.axis_size("blk"), lax.axis_size("group")
    n_col = next(k for k in range(math.isqrt(n_group), 0, -1) if n_group % k == 0)
    n_row = n_group // n_col
    shape = jax.ShapeDtypeStruct
    parts = 8 if width % 1024 == 0 else 1

    def kernel(body, flops, moved, **options):
        return pl.pallas_call(
            body,
            cost_estimate=pl.CostEstimate(flops=flops, bytes_accessed=moved, transcendentals=0),
            compiler_params=pltpu.CompilerParams(vmem_limit_bytes=16 * 2**20),
            **options,
        )

    side = n_col if n_row == n_col else 0

    def route(image_side, distance, k):
        pairs = []
        for i in range(n_blk):
            j = (i + distance) % n_blk
            along_row = image_side if side == 0 or j % 2 == 1 else not image_side
            for g in range(n_group):
                r, c = g // n_col, g % n_col
                r, c = (r, (c + k) % n_col) if along_row else ((r + k) % n_row, c)
                pairs.append((i * n_group + g, j * n_group + r * n_col + c))
        return pairs

    def send(piece, image_side, distance, k):
        return lax.ppermute(piece, ("blk", "group"), route(image_side, distance, k))

    first = lax.broadcasted_iota(jnp.int32, (8, 128), 0) == 0
    scalars = jnp.where(first, jnp.exp(natural_exponent_factor[0]), bias[0])

    unit_shapes = (shape((rows, emb), F32), shape((rows, 1), F32), shape((rows, emb), BF16))
    early = kernel(
        mark_kernel, 40 * rows * width * emb, 20 * width * (rows + emb), out_shape=shape((8, 128), F32), out_specs=VMEM
    )()
    earlier_texts = [send(text_emb, False, 1, k) for k in range(n_row)]
    texts = [text_emb] + [send(text_emb, False, 0, k) for k in range(1, n_row)]

    img_unit, img_inv, img_low = kernel(
        project_kernel,
        2 * rows * width * emb,
        2 * width * (rows + emb),
        out_shape=unit_shapes,
        in_specs=[ANY] + [VMEM] * 2,
        out_specs=(VMEM,) * 3,
    )(early, img_feat, head_weight)

    images = [img_low] + [send(img_low, True, 0, k) for k in range(1, n_col)]
    later_images = [send(img_low, True, -1, k) for k in range(n_col)]

    low_piece, grad_piece = shape((rows, emb), BF16), shape((rows, emb), F32)
    earlier_lows, after = [], scalars
    for piece in earlier_texts:
        after = kernel(
            low_kernel,
            8 * rows * emb,
            4 * rows * emb,
            out_shape=low_piece,
            in_specs=[VMEM, ANY],
            out_specs=VMEM,
        )(piece, after)
        earlier_lows.append(after)

    grad_img, *img_terms = kernel(
        functools.partial(image_kernel, n_col, n_row),
        8 * n_col * n_row * rows * rows * emb,
        2 * rows * emb * (2 * n_col + 3 * n_row),
        out_shape=(grad_piece,) + (low_piece,) * (n_col - 1),
        in_specs=[VMEM] + [ANY] * n_row + [VMEM] * (n_col + 2 * n_row),
        out_specs=(VMEM,) * n_col,
        scratch_shapes=[pltpu.VMEM((n_col * rows, 2 * n_row * rows), BF16)],
    )(scalars, *earlier_texts, *images, *texts, *earlier_lows)
    img_peers = [send(term, True, 0, -k) for k, term in enumerate(img_terms, 1)]

    grad_txt, *txt_terms = kernel(
        functools.partial(text_kernel, n_row, 2 * n_col),
        8 * n_col * n_row * rows * rows * emb,
        2 * rows * emb * (2 * n_col + 3 * n_row),
        out_shape=(grad_piece,) + (low_piece,) * (n_row - 1),
        in_specs=[VMEM] * (1 + n_row + 2 * n_col),
        out_specs=(VMEM,) * n_row,
        scratch_shapes=[pltpu.VMEM((n_row * rows, 2 * n_col * rows), BF16)],
    )(scalars, *texts, *images, *later_images)
    txt_peers = [send(term, False, 0, -k) for k, term in enumerate(txt_terms, 1)]

    d_feat, txt_unit, txt_inv = kernel(
        feat_kernel,
        2 * rows * width * emb,
        4 * width * (rows + emb),
        out_shape=(shape((rows, width), F32), grad_piece, shape((rows, 1), F32)),
        in_specs=[VMEM] * (5 + len(img_peers)),
        out_specs=(HBM, VMEM, VMEM),
        scratch_shapes=[pltpu.VMEM((rows, width), F32), pltpu.SemaphoreType.DMA((parts,))],
    )(grad_img, img_unit, img_inv, head_weight, text_emb, *img_peers)

    d_text = kernel(
        text_out_kernel,
        8 * rows * emb,
        12 * rows * emb,
        out_shape=shape((rows, emb), F32),
        in_specs=[VMEM] * (3 + len(txt_peers)),
        out_specs=VMEM,
    )(grad_txt, txt_unit, txt_inv, *txt_peers)
    return d_feat, d_text


def solution(mesh):
    return jax.shard_map(
        body,
        mesh=mesh,
        in_specs=(P(("blk", "group"), None), P(), P(("blk", "group"), None), P(), P()),
        out_specs=(P(("blk", "group"), None), P(("blk", "group"), None)),
        check_vma=False,
    )
```
